512 devices in a mesh: region: 128 (over z, y, core), sub: 4 (over x).
Axes of the slice: x: 4, y: 8, z: 8, core: 2. Of those that a mesh axis runs over, the one named last changes fastest.
Arguments:
- modal_state: float32 [9, 56, 65536], P(None, None, ('region', 'sub')), may hold values from -6 to 6
- deriv_stiff: float32 [3, 56, 56], replicated, may hold values from -0.75 to 0.75
- volume_stiff: float32 [3, 56, 56], replicated, may hold values from -0.5 to 0.5
- local_flux: float32 [4, 56, 56], replicated, may hold values from -0.375 to 0.375
- neighbour_flux: float32 [4, 12, 56, 56], replicated, may hold values from -0.375 to 0.375
- star_matrices: float32 [3, 9, 9, 65536], P(None, None, None, ('region', 'sub')), may hold values from -2 to 2
- plus_flux: float32 [4, 9, 9, 65536], P(None, None, None, ('region', 'sub')), may hold values from -2 to 2
- minus_flux: float32 [4, 9, 9, 65536], P(None, None, None, ('region', 'sub')), may hold values from -2 to 2
- cluster_ids: int32 [65536], P(('region', 'sub')), may hold values from 0 to 2
- face_neighbours: int32 [4, 65536], P(None, ('region', 'sub')), may hold values from 0 to 287
- face_orient: int32 [4, 65536], P(None, ('region', 'sub')), may hold values from 0 to 11
- send_lists: int32 [512, 4, 3, 32], P(('region', 'sub')), may hold values from 0 to 127
- sub_lists: int32 [512, 3, 8], P(('region', 'sub')), may hold values from 0 to 127
Outputs:
- new_state: float32 [9, 56, 65536], P(None, None, ('region', 'sub'))
The draws below stay inside these ranges and needn't reach their ends.
Inputs may be any that keep to these rules, and one draw needn't show every extreme that they name: `face_neighbours`: values below 128 name elements of the same partition, the next 128 name slots received from neighbouring regions, the last 32 slots received from the region's subpartitions. `send_lists`: every slot of every list is used. `sub_lists`: every slot of every list is used.
All inputs are finite; a program needn't handle non-finite values.
Results may differ from the reference program's by a relative error of at most 0.0003.
Values sent between devices are 32-bit elements; how exact they have to be, the bound alone decides.
A program may use at most 128 MiB of HBM per device.

```python
import jax
import jax.numpy as jnp
from jax import lax

M = 56
NQ = 9
NDER = 6
NCLUS = 3
ORIENT = 12
E_DEV = 128
SLOT = 32
SLOT_SUB = 8
DEVICES_ALL = 512
ELEMS = 65536
N_REGION = 128
N_SUB = 4


def with_ends(drawn, rng, least, high):
    extent = drawn.shape
    index_at = [jax.random.randint(jax.random.fold_in(rng, axis), (), 0, extent[axis]) for axis in range(len(extent))]
    drawn = drawn.at[tuple(index_at)].set(least)
    longest = extent.index(max(extent))
    index_at[longest] = (index_at[longest] + 1) % extent[longest]
    return drawn.at[tuple(index_at)].set(high)


def block_levels(rng, dims, shards, smallest, high):
    def one(dim, shards_of):
        draws = jax.random.uniform(jax.random.fold_in(jax.random.fold_in(rng, 6), dim), (shards_of,), jnp.float32, smallest / len(shards), high / len(shards))
        return jnp.repeat(jnp.exp(draws), dims[dim] // shards_of).reshape((-1,) + (1,) * (len(dims) - dim - 1))

    loudness = one(*shards[0])
    for cut in shards[1:]:
        loudness = loudness * one(*cut)
    return loudness


def noise(rng, dims, scale, bound, shards=(), kind=jnp.bfloat16):
    entries = jax.random.normal(rng, dims, jnp.float32) * scale
    if len(shards) > 0:
        entries = block_levels(rng, dims, shards, -0.22, 0.18) * entries
    return jnp.clip(entries, min=-bound, max=bound).astype(kind)


def setup_inputs(seed: int = 0) -> dict:
    key_list = jax.random.split(jax.random.key(seed), 14)
    return {
        "modal_state": noise(key_list[0], (NQ, M, ELEMS), 1.0, 6.0, ((2, 512),), jnp.float32),
        "deriv_stiff": noise(key_list[1], (3, M, M), M ** -0.5, 0.75, (), jnp.float32),
        "volume_stiff": noise(key_list[2], (3, M, M), (3 * M) ** -0.5, 0.5, (), jnp.float32),
        "local_flux": noise(key_list[3], (4, M, M), (4 * M) ** -0.5, 0.375, (), jnp.float32),
        "neighbour_flux": noise(key_list[4], (4, ORIENT, M, M), (4 * M) ** -0.5, 0.375, (), jnp.float32),
        "star_matrices": noise(key_list[5], (3, NQ, NQ, ELEMS), NQ ** -0.5, 2.0, ((3, 512),), jnp.float32),
        "plus_flux": noise(key_list[6], (4, NQ, NQ, ELEMS), NQ ** -0.5, 2.0, ((3, 512),), jnp.float32),
        "minus_flux": noise(key_list[7], (4, NQ, NQ, ELEMS), NQ ** -0.5, 2.0, ((3, 512),), jnp.float32),
        "cluster_ids": with_ends(jax.random.randint(key_list[8], (ELEMS,), 0, NCLUS), jax.random.fold_in(key_list[8], 1), 0, NCLUS - 1).astype(jnp.int32),
        "face_neighbours": with_ends(jax.random.randint(key_list[9], (4, ELEMS), 0, E_DEV + 4 * SLOT + N_SUB * SLOT_SUB), jax.random.fold_in(key_list[9], 1), 0, (E_DEV + 4 * SLOT + N_SUB * SLOT_SUB) - 1).astype(jnp.int32),
        "face_orient": with_ends(jax.random.randint(key_list[10], (4, ELEMS), 0, ORIENT), jax.random.fold_in(key_list[10], 1), 0, ORIENT - 1).astype(jnp.int32),
        "send_lists": with_ends(jax.random.randint(key_list[11], (DEVICES_ALL, 4, NCLUS, SLOT), 0, E_DEV), jax.random.fold_in(key_list[11], 1), 0, E_DEV - 1).astype(jnp.int32),
        "sub_lists": with_ends(jax.random.randint(key_list[12], (DEVICES_ALL, NCLUS, SLOT_SUB), 0, E_DEV), jax.random.fold_in(key_list[12], 1), 0, E_DEV - 1).astype(jnp.int32),
    }


base_step = 0.25


def apply_small(matrix, values):
    running = matrix[:, 0, :][:, None, :] * values[0][None, :, :]
    for column in range(1, values.shape[0]):
        running = running + matrix[:, column, :][:, None, :] * values[column][None, :, :]
    return running


def apply_modes(matrix, values):
    return jnp.einsum("mn,qne->qme", matrix, values, precision=lax.Precision.HIGHEST, preferred_element_type=jnp.float32)


def predict(start_state, stars, deriv_stiff):
    series = [start_state]
    current = start_state
    for deriv_order in range(NDER - 1):
        running = jnp.zeros_like(current)
        for direction in range(3):
            running = running + apply_small(stars[direction], apply_modes(deriv_stiff[direction], current))
        current = -running
        series.append(current)
    results = []
    for cluster in range(NCLUS):
        step_width = base_step * 2.0 ** cluster
        running = jnp.zeros_like(start_state)
        factor = 1.0
        for deriv_order in range(NDER):
            factor = factor * step_width / (deriv_order + 1)
            running = running + factor * series[deriv_order]
        results.append(running)
    return jnp.stack(results)


def reference(modal_state, deriv_stiff, volume_stiff, local_flux, neighbour_flux, star_matrices, plus_flux, minus_flux, cluster_ids, face_neighbours, face_orient, send_lists, sub_lists):
    local_count = E_DEV
    partitions = N_REGION * N_SUB
    region_slots = 4 * SLOT

    def predict_device(device):
        start = device * local_count
        start_state = lax.dynamic_slice_in_dim(modal_state, start, local_count, 2)
        stars = lax.dynamic_slice_in_dim(star_matrices, start, local_count, 3)
        return predict(start_state, stars, deriv_stiff)

    integrals = lax.map(predict_device, jnp.arange(partitions, dtype=jnp.int32))
    offsets = jnp.array([-2, -1, 1, 2], dtype=jnp.int32)

    def update_device(device):
        start = device * local_count
        region = device // N_SUB
        sub_index = device % N_SUB
        start_state = lax.dynamic_slice_in_dim(modal_state, start, local_count, 2)
        stars = lax.dynamic_slice_in_dim(star_matrices, start, local_count, 3)
        plus_side = lax.dynamic_slice_in_dim(plus_flux, start, local_count, 3)
        minus_side = lax.dynamic_slice_in_dim(minus_flux, start, local_count, 3)
        clusters = lax.dynamic_slice_in_dim(cluster_ids, start, local_count, 0)
        neighbours = lax.dynamic_slice_in_dim(face_neighbours, start, local_count, 1)
        orients = lax.dynamic_slice_in_dim(face_orient, start, local_count, 1)
        local_all = integrals[device]
        own_integral = jnp.zeros_like(start_state)
        for cluster in range(NCLUS):
            own_integral = jnp.where(clusters[None, None, :] == cluster, local_all[cluster], own_integral)
        result = start_state
        for direction in range(3):
            result = result + apply_small(stars[direction], apply_modes(volume_stiff[direction], own_integral))
        for face_index in range(4):
            result = result - apply_small(plus_side[face_index], apply_modes(local_flux[face_index], own_integral))
            neighbour_entry = neighbours[face_index]
            is_local = neighbour_entry < local_count
            is_region = (neighbour_entry >= local_count) & (neighbour_entry < local_count + region_slots)
            region_pos = jnp.clip(neighbour_entry - local_count, 0, region_slots - 1)
            block_index = region_pos // SLOT
            slot_index = region_pos % SLOT
            source_region = (region + offsets[block_index]) % N_REGION
            region_device = source_region * N_SUB + sub_index
            region_element = send_lists[region_device, 3 - block_index, clusters, slot_index]
            sub_pos = jnp.clip(neighbour_entry - local_count - region_slots, 0, N_SUB * SLOT_SUB - 1)
            sub_device = region * N_SUB + sub_pos // SLOT_SUB
            sub_element = sub_lists[sub_device, clusters, sub_pos % SLOT_SUB]
            source_device = jnp.where(is_local, device, jnp.where(is_region, region_device, sub_device)).astype(jnp.int32)
            source_element = jnp.where(is_local, jnp.clip(neighbour_entry, 0, local_count - 1), jnp.where(is_region, region_element, sub_element)).astype(jnp.int32)
            gathered = integrals[source_device, clusters, :, :, source_element]
            partner = jnp.transpose(gathered, (1, 2, 0))
            mixed = apply_small(minus_side[face_index], partner)
            selected = jnp.zeros_like(mixed)
            for orient_id in range(ORIENT):
                selected = jnp.where(orients[face_index][None, None, :] == orient_id, apply_modes(neighbour_flux[face_index, orient_id], mixed), selected)
            result = result - selected
        return result

    updated = lax.map(update_device, jnp.arange(partitions, dtype=jnp.int32))
    return jnp.transpose(updated, (1, 2, 0, 3)).reshape(NQ, M, partitions * local_count)
```

```python
import functools

import jax
import jax.numpy as jnp
from jax import lax
from jax.experimental import pallas as pl
from jax.experimental.pallas import tpu as pltpu
from jax.sharding import PartitionSpec as P

MESH = pl.DeviceIdType.MESH
F32, BF16 = jnp.float32, jnp.bfloat16

NDER = 6
NCLUS = 3
BASE_STEP = 0.25
OFFSETS = (-2, -1, 1, 2)
M = 56
NQ = 9
E = 128
SLOT = 32
SSUB = 8
NORI = 12
ROWS = 512
REG = NCLUS * SLOT
SUB = NCLUS * SSUB
NCH = 4
TAYLOR = []
for _c in range(NCLUS):
    _factor, _row = 1.0, []
    for _k in range(NDER):
        _factor = _factor * (BASE_STEP * 2.0**_c) / (_k + 1)
        _row.append(_factor)
    TAYLOR.append(_row)


def pieces(x):
    high = x.astype(BF16).astype(F32)
    return high, x - high


def left_stack(a):
    high, low = pieces(a)
    gap = jnp.zeros((a.shape[0], 8), F32)
    return jnp.concatenate([high, gap, high, gap, low, gap, low, gap], axis=1).astype(BF16)


def right_slots(high, low):
    gap = jnp.zeros((8, high.shape[1]), F32)
    half = jnp.concatenate([high, gap, low, gap], axis=0).astype(BF16)
    return jnp.concatenate([half, half], axis=0)


def right_stack(x):
    return right_slots(*pieces(x))


def mm(a, b):
    return jnp.dot(a, b, preferred_element_type=F32)


def body(
    n_region, n_sub,
    state_h, dstiff_h, vstiff_h, lflux_h, nflux_h, star_h, plus_h, minus_h,
    clus_h, nbr_h, orient_h, slist_h, blist_h,
    out_h,
    state, dstiff, vstiff, lflux, nflux, star, plus, minus, clus, nbr, orient, slist, blist,
    dstack, wstack, nstack, xs, ys, integ, ihl, tmp, esel, ohl, ohg, own_y, part, sel, res,
    sbuf, sbsub, gbuf,
    in_sem, out_sem, send_sem, recv_sem, ssend_sem, srecv_sem,
):
    r = lax.axis_index("region")
    s = lax.axis_index("sub")
    regions = [lax.rem(r + (o + n_region), n_region) for o in OFFSETS]
    subs = [lax.rem(s + d, n_sub) for d in range(n_sub)]

    barrier = pltpu.get_barrier_semaphore()
    for j in regions:
        pl.semaphore_signal(barrier, inc=1, device_id=(j, s), device_id_type=MESH)
    for d in range(1, n_sub):
        pl.semaphore_signal(barrier, inc=1, device_id=(r, subs[d]), device_id_type=MESH)

    loads = {}
    for i, (name, src, dst) in enumerate((
        ("dstiff", dstiff_h, dstiff), ("state", state_h, state), ("star", star_h, star),
        ("slist", slist_h, slist), ("blist", blist_h, blist), ("clus", clus_h, clus),
        ("nbr", nbr_h, nbr), ("orient", orient_h, orient), ("vstiff", vstiff_h, vstiff),
        ("lflux", lflux_h, lflux), ("plus", plus_h, plus), ("nflux", nflux_h, nflux),
        ("minus", minus_h, minus),
    )):
        loads[name] = pltpu.make_async_copy(src, dst, in_sem.at[i])
        loads[name].start()

    groups = ((0, 1), (2, 3), (4, 5), (6, 7), (8,))

    integ[:, NQ * M :, :] = jnp.zeros((NCLUS, ROWS - NQ * M, E), F32)
    gbuf[:, 4 * REG + n_sub * SUB :, :] = jnp.zeros((NCH, 512 - 4 * REG - n_sub * SUB, E), F32)

    loads["dstiff"].wait()
    dstack[...] = left_stack(-dstiff[...].reshape(3 * M, M))

    loads["state"].wait()

    def modes(source, target):
        for group in groups:
            y = mm(dstack[...], jnp.concatenate([right_stack(source[q]) for q in group], axis=1))
            for i, q in enumerate(group):
                target[q] = y[:, E * i : E * (i + 1)]

    modes(state, ys)
    for q in range(NQ):
        x = state[q]
        for c in range(NCLUS):
            integ[c, M * q : M * (q + 1), :] = TAYLOR[c][0] * x

    def apply_star(ps):
        acc = [None] * len(ps)
        for q in range(NQ):
            for d in range(3):
                y = ys[q, M * d : M * (d + 1), :]
                for i, p in enumerate(ps):
                    term = star[d, p, q : q + 1, :] * y
                    acc[i] = term if acc[i] is None else acc[i] + term
        return acc

    loads["star"].wait()
    for k in range(1, NDER - 1):
        for ps in ((0, 1, 2), (3, 4, 5), (6, 7, 8)):
            for p, x in zip(ps, apply_star(ps)):
                xs[p] = x
                for c in range(NCLUS):
                    integ[c, M * p : M * (p + 1), :] += TAYLOR[c][k] * x
        modes(xs, ys)

    loads["slist"].wait()
    loads["blist"].wait()
    tmp[...] = jnp.zeros((E, E), F32)
    for o in range(4):
        tmp[8 * o : 8 * o + NCLUS, 0:SLOT] = slist[0, o].astype(F32)
    tmp[32 : 32 + NCLUS, 0:SSUB] = blist[0].astype(F32)
    lists = tmp[...].T
    lane = lax.broadcasted_iota(jnp.int32, (SLOT, E), 1).astype(F32)
    for c in range(NCLUS):
        rows = [
            jnp.where(lists[0:SLOT, 8 * o + c : 8 * o + c + 1] == lane, 1.0, 0.0) for o in range(4)
        ]
        rows.append(jnp.where(lists[0:SSUB, 32 + c : 33 + c] == lane[0:SSUB], 1.0, 0.0))
        rows.append(jnp.zeros((8, E), F32))
        onehot = jnp.concatenate(rows, axis=0).astype(BF16)
        esel[c] = jnp.concatenate([onehot, onehot], axis=1)

    pl.semaphore_wait(barrier, 4 + n_sub - 1)

    sends = []

    def send_chunk(i):
        span = slice(E * i, E * (i + 1))
        for c in range(NCLUS):
            high, low = pieces(integ[c, span, :])
            ihl[c, span, :] = jnp.concatenate([high, low], axis=1).astype(BF16)
            picked = lax.dot_general(
                esel[c], ihl[c, span, :], (((1,), (1,)), ((), ())), preferred_element_type=F32
            )
            for o in range(4):
                sbuf[i, o, SLOT * c : SLOT * (c + 1), :] = picked[SLOT * o : SLOT * (o + 1)]
            sbsub[i, SSUB * c : SSUB * (c + 1), :] = picked[4 * SLOT : 4 * SLOT + SSUB]
        for o in (0, 3, 1, 2):
            b = 3 - o
            copy = pltpu.make_async_remote_copy(
                src_ref=sbuf.at[i, o],
                dst_ref=gbuf.at[i, pl.ds(REG * b, REG), :],
                send_sem=send_sem.at[i, o],
                recv_sem=recv_sem.at[i, b],
                device_id=(regions[o], s),
                device_id_type=MESH,
            )
            copy.start()
            sends.append(copy)
        for d in range(1, n_sub):
            copy = pltpu.make_async_remote_copy(
                src_ref=sbsub.at[i],
                dst_ref=gbuf.at[i, pl.ds(4 * REG + SUB * d, SUB), :],
                send_sem=ssend_sem.at[i, d],
                recv_sem=srecv_sem.at[i, d],
                device_id=(r, subs[d]),
                device_id_type=MESH,
            )
            copy.start()
            sends.append(copy)
        gbuf[i, 4 * REG : 4 * REG + SUB, :] = sbsub[i]

    k = NDER - 1
    for i, ps in enumerate(((0, 1, 2), (3, 4), (5, 6), (7, 8))):
        for p, x in zip(ps, apply_star(ps)):
            for c in range(NCLUS):
                integ[c, M * p : M * (p + 1), :] += TAYLOR[c][k] * x
        send_chunk(i)

    for name in ("clus", "nbr", "orient", "vstiff", "lflux", "plus"):
        loads[name].wait()
    wstack[...] = left_stack(
        jnp.concatenate([vstiff[...].reshape(3 * M, M), -lflux[...].reshape(4 * M, M)], axis=0)
    )
    cl = clus[...]
    for group in groups:
        columns = []
        for q in group:
            span = slice(M * q, M * (q + 1))
            own = jnp.where(
                cl == 0, integ[0, span, :], jnp.where(cl == 1, integ[1, span, :], integ[2, span, :])
            )
            columns.append(right_stack(own))
        y = mm(wstack[...], jnp.concatenate(columns, axis=1))
        for i, q in enumerate(group):
            own_y[q] = y[:, E * i : E * (i + 1)]
    for ps in ((0, 1, 2), (3, 4, 5), (6, 7, 8)):
        acc = [state[p] for p in ps]
        for q in range(NQ):
            for j in range(7):
                y = own_y[q, M * j : M * (j + 1), :]
                for i, p in enumerate(ps):
                    weight = star[j, p, q : q + 1, :] if j < 3 else plus[j - 3, p, q : q + 1, :]
                    acc[i] = acc[i] + weight * y
        for i, p in enumerate(ps):
            res[p] = acc[i]

    row_l = lax.broadcasted_iota(jnp.int32, (NCLUS * E, E), 0)
    row_g = lax.broadcasted_iota(jnp.int32, (512, E), 0)
    for f in range(4):
        v = nbr[f : f + 1, :]
        at_region = v - E
        at_sub = v - 2 * E
        k_region = (at_region >> 5) * REG + cl * SLOT + (at_region & 31)
        k_sub = 4 * REG + ((s - (at_sub >> 3)) & 3) * SUB + cl * SSUB + (at_sub & 7)
        k_local = jnp.where(v < E, cl * E + v, -1)
        k_ghost = jnp.where(v < E, -1, jnp.where(v < 2 * E, k_region, k_sub))
        span = slice(E * f, E * (f + 1))
        ohl[:, span] = jnp.where(row_l == k_local, 1.0, 0.0).astype(BF16)
        ohg[:, span] = jnp.where(row_g == k_ghost, 1.0, 0.0).astype(BF16)

    for i in range(NCH):
        span = slice(E * i, E * (i + 1))
        high = jnp.concatenate([ihl[c, span, 0:E] for c in range(NCLUS)], axis=1)
        low = jnp.concatenate([ihl[c, span, E:] for c in range(NCLUS)], axis=1)
        part[i] = mm(jnp.concatenate([high, low], axis=0), ohl[...])

    loads["nflux"].wait()
    for f in range(4):
        for j in range(NORI // 2):
            pair = nflux[f, 2 * j : 2 * j + 2].reshape(2 * M, M)
            nstack[f, 2 * M * j : 2 * M * (j + 1), :] = left_stack(-pair)
    loads["minus"].wait()

    def partner(h, q, f):
        got, row, end = [], M * q, M * (q + 1)
        while row < end:
            i = row // E
            stop = min(end, E * (i + 1))
            lo = row - E * i + E * h
            got.append(part[i, lo : lo + stop - row, E * f : E * (f + 1)])
            row = stop
        return got[0] if len(got) == 1 else jnp.concatenate(got, axis=0)

    todo = (((0, 1),), ((2, 3),), ((4, 5),), ((6, 7), (8,)))
    for i in range(NCH):
        for o in range(4):
            b = 3 - o
            pltpu.make_async_remote_copy(
                src_ref=sbuf.at[i, o], dst_ref=gbuf.at[i, pl.ds(REG * b, REG), :],
                send_sem=send_sem.at[i, o], recv_sem=recv_sem.at[i, b],
                device_id=(regions[o], s), device_id_type=MESH,
            ).wait_recv()
        for d in range(1, n_sub):
            pltpu.make_async_remote_copy(
                src_ref=sbsub.at[i], dst_ref=gbuf.at[i, pl.ds(4 * REG + SUB * d, SUB), :],
                send_sem=ssend_sem.at[i, d], recv_sem=srecv_sem.at[i, d],
                device_id=(r, subs[d]), device_id_type=MESH,
            ).wait_recv()
        high, low = pieces(gbuf[i].T)
        part[i] += mm(jnp.concatenate([high, low], axis=0).astype(BF16), ohg[...])
        for group in todo[i]:
            for f in range(4):
                columns = [right_slots(partner(0, q, f), partner(1, q, f)) for q in group]
                every = mm(nstack[f], jnp.concatenate(columns, axis=1))
                face = orient[f : f + 1, :]
                for j in range(len(group)):
                    span = slice(E * j, E * (j + 1))
                    chosen = every[0:M, span]
                    for o in range(1, NORI):
                        chosen = jnp.where(face == o, every[M * o : M * (o + 1), span], chosen)
                    sel[len(group) * f + j] = chosen
            last = group == (8,)
            for ps in ((0, 1, 2), (3, 4, 5), (6, 7, 8)):
                acc = [res[p] for p in ps]
                for f in range(4):
                    for j, q in enumerate(group):
                        y = sel[len(group) * f + j]
                        for n, p in enumerate(ps):
                            acc[n] = acc[n] + minus[f, p, q : q + 1, :] * y
                for n, p in enumerate(ps):
                    res[p] = acc[n]
                if last:
                    span = pl.ds(ps[0], len(ps))
                    pltpu.make_async_copy(res.at[span], out_h.at[span], out_sem.at[ps[0] // 3]).start()

    for n in range(3):
        span = pl.ds(3 * n, 3)
        pltpu.make_async_copy(res.at[span], out_h.at[span], out_sem.at[n]).wait()
    for copy in sends:
        copy.wait_send()


def local(n_region, n_sub, state, dstiff, vstiff, lflux, nflux, star, plus, minus, clus, nbr, orient, slist, blist):
    clus = clus.reshape(1, E)
    args = (state, dstiff, vstiff, lflux, nflux, star, plus, minus, clus, nbr, orient, slist, blist)
    vm = pltpu.VMEM
    return pl.pallas_call(
        functools.partial(body, n_region, n_sub),
        out_shape=jax.ShapeDtypeStruct((NQ, M, E), F32),
        in_specs=[pl.BlockSpec(memory_space=pl.ANY)] * len(args),
        out_specs=pl.BlockSpec(memory_space=pl.ANY),
        scratch_shapes=[vm(a.shape, a.dtype) for a in args]
        + [
            vm((3 * M, 256), BF16),
            vm((7 * M, 256), BF16),
            vm((4, NORI * M, 256), BF16),
            vm((NQ, M, E), F32),
            vm((NQ, 3 * M, E), F32),
            vm((NCLUS, ROWS, E), F32),
            vm((NCLUS, ROWS, 2 * E), BF16),
            vm((E, E), F32),
            vm((NCLUS, 144, 2 * E), BF16),
            vm((NCLUS * E, 4 * E), BF16),
            vm((512, 4 * E), BF16),
            vm((NQ, 7 * M, E), F32),
            vm((NCH, 2 * E, 4 * E), F32),
            vm((8, M, E), F32),
            vm((NQ, M, E), F32),
            vm((NCH, 4, REG, E), F32),
            vm((NCH, SUB, E), F32),
            vm((NCH, 512, E), F32),
            pltpu.SemaphoreType.DMA((len(args),)),
            pltpu.SemaphoreType.DMA((3,)),
            pltpu.SemaphoreType.DMA((NCH, 4)),
            pltpu.SemaphoreType.DMA((NCH, 4)),
            pltpu.SemaphoreType.DMA((NCH, n_sub)),
            pltpu.SemaphoreType.DMA((NCH, n_sub)),
        ],
        compiler_params=pltpu.CompilerParams(
            collective_id=0, has_side_effects=True, vmem_limit_bytes=44 * 2**20
        ),
        cost_estimate=pl.CostEstimate(flops=2_000_000_000, bytes_accessed=4_000_000, transcendentals=0),
        name="ader_step",
    )(*args)


def solution(mesh):
    return jax.shard_map(
        functools.partial(local, mesh.shape["region"], mesh.shape["sub"]),
        mesh=mesh,
        in_specs=(
            P(None, None, ("region", "sub")),
            P(),
            P(),
            P(),
            P(),
            P(None, None, None, ("region", "sub")),
            P(None, None, None, ("region", "sub")),
            P(None, None, None, ("region", "sub")),
            P(("region", "sub")),
            P(None, ("region", "sub")),
            P(None, ("region", "sub")),
            P(("region", "sub"), None, None, None),
            P(("region", "sub"), None, None),
        ),
        out_specs=P(None, None, ("region", "sub")),
        check_vma=False,
    )
```

```python
import functools

import jax
import jax.numpy as jnp
from jax import lax
from jax.experimental import pallas as pl
from jax.experimental.pallas import tpu as pltpu
from jax.sharding import PartitionSpec as P

MESH = pl.DeviceIdType.MESH
F32, BF16 = jnp.float32, jnp.bfloat16

NDER = 6
NCLUS = 3
BASE_STEP = 0.25
OFFSETS = (-2, -1, 1, 2)
M = 56
NQ = 9
E = 128
SLOT = 32
SSUB = 8
NORI = 12
ROWS = 512
REG = NCLUS * SLOT
SUB = NCLUS * SSUB
FROM = 4 * REG + 3 * SUB
NCH = 4
TAYLOR = []
for _c in range(NCLUS):
    _factor, _row = 1.0, []
    for _k in range(NDER):
        _factor = _factor * (BASE_STEP * 2.0**_c) / (_k + 1)
        _row.append(_factor)
    TAYLOR.append(_row)


def pieces(x):
    high = x.astype(BF16).astype(F32)
    return high, x - high


def left_stack(a):
    high, low = pieces(a)
    gap = jnp.zeros((a.shape[0], 8), F32)
    return jnp.concatenate([high, gap, high, gap, low, gap, low, gap], axis=1).astype(BF16)


def right_slots(high, low):
    gap = jnp.zeros((8, high.shape[1]), F32)
    half = jnp.concatenate([high, gap, low, gap], axis=0).astype(BF16)
    return jnp.concatenate([half, half], axis=0)


def right_stack(x):
    return right_slots(*pieces(x))


def mm(a, b):
    return jnp.dot(a, b, preferred_element_type=F32)


def body(
    n_region, n_sub,
    state_h, dstiff_h, vstiff_h, lflux_h, nflux_h, star_h, plus_h, minus_h,
    clus_h, nbr_h, orient_h, slist_h, blist_h,
    res,
    state, dstiff, vstiff, lflux, nflux, star, plus, minus, clus, nbr, orient, slist, blist,
    dstack, wstack, nstack, ys, ys2, integ, ihl, tmp, esel, ohl, ohg, own_y, part, sel,
    sbuf, sbsub, gbuf,
    in_sem, send_sem, recv_sem,
):
    r = lax.axis_index("region")
    s = lax.axis_index("sub")
    regions = [lax.rem(r + (o + n_region), n_region) for o in OFFSETS]
    subs = [lax.rem(s + d, n_sub) for d in range(n_sub)]

    barrier = pltpu.get_barrier_semaphore()
    for j in regions:
        pl.semaphore_signal(barrier, inc=1, device_id=(j, s), device_id_type=MESH)
    for d in range(1, n_sub):
        pl.semaphore_signal(barrier, inc=1, device_id=(r, subs[d]), device_id_type=MESH)

    loads = {}
    for i, (name, src, dst) in enumerate((
        ("dstiff", dstiff_h, dstiff), ("state", state_h, state), ("star", star_h, star),
        ("slist", slist_h, slist), ("blist", blist_h, blist),
        ("vstiff", vstiff_h, vstiff),
        ("clus", clus_h, clus), ("nbr", nbr_h, nbr), ("orient", orient_h, orient),
        ("lflux", lflux_h, lflux), ("plus", plus_h, plus), ("nflux", nflux_h, nflux),
        ("minus", minus_h, minus),
    )):
        loads[name] = pltpu.make_async_copy(src, dst, in_sem.at[i])
        if i < 5:
            loads[name].start()

    late = ("vstiff", "clus", "nbr", "orient", "lflux", "plus", "nflux", "minus")
    groups = ((0, 1), (2, 3), (4, 5), (6, 7), (8,))

    integ[:, NQ * M :, :] = jnp.zeros((NCLUS, ROWS - NQ * M, E), F32)
    gbuf[:, 4 * REG + n_sub * SUB :, :] = jnp.zeros((NCH, 512 - 4 * REG - n_sub * SUB, E), F32)

    loads["dstiff"].wait()
    dstack[...] = left_stack(-dstiff[...].reshape(3 * M, M))

    loads["state"].wait()

    pairs = ((0, 1), (2, 3), (4, 5), (6, 7), (8,))

    def modes(group, values, target):
        y = mm(dstack[...], jnp.concatenate([right_stack(x) for x in values], axis=1))
        for i, q in enumerate(group):
            target[q] = y[:, E * i : E * (i + 1)]

    for group in pairs:
        modes(group, [state[q] for q in group], ys)
    for q in range(NQ):
        x = state[q]
        for c in range(NCLUS):
            integ[c, M * q : M * (q + 1), :] = TAYLOR[c][0] * x

    def apply_star(ps, source):
        acc = [None] * len(ps)
        for q in range(NQ):
            for d in range(3):
                y = source[q, M * d : M * (d + 1), :]
                for i, p in enumerate(ps):
                    term = star[p, q, d : d + 1, :] * y
                    acc[i] = term if acc[i] is None else acc[i] + term
        return acc

    loads["slist"].wait()
    loads["blist"].wait()
    tmp[...] = jnp.zeros((E, E), F32)
    for c in range(NCLUS):
        tmp[8 * c : 8 * c + 4, 0:SLOT] = slist[c].astype(F32)
        tmp[8 * c + 4 : 8 * c + 5, 0:SSUB] = blist[c].astype(F32)
    lists = tmp[...].T
    lane = lax.broadcasted_iota(jnp.int32, (SLOT, E), 1).astype(F32)
    for c in range(NCLUS):
        rows = [
            jnp.where(lists[0:SLOT, 8 * c + o : 8 * c + o + 1] == lane, 1.0, 0.0) for o in range(4)
        ]
        rows.append(jnp.where(lists[0:SSUB, 8 * c + 4 : 8 * c + 5] == lane[0:SSUB], 1.0, 0.0))
        rows.append(jnp.zeros((8, E), F32))
        onehot = jnp.concatenate(rows, axis=0).astype(BF16)
        esel[c] = jnp.concatenate([onehot, onehot], axis=1)

    loads["star"].wait()
    for name in late:
        loads[name].start()

    def step(k, source, target):
        weights = []
        for c in range(NCLUS):
            weights.append(TAYLOR[c][k])
        for group in ((0, 1, 2), (3, 4, 5), (6, 7, 8)):
            xs = apply_star(group, source)
            modes(group, xs, target)
            for p, x in zip(group, xs):
                for c in range(NCLUS):
                    integ[c, M * p : M * (p + 1), :] += weights[c] * x

    def two_steps(n, carry):
        step(2 * n + 1, ys, ys2)
        step(2 * n + 2, ys2, ys)
        return carry

    two_steps(0, 0)
    two_steps(1, 0)

    pl.semaphore_wait(barrier, 4 + n_sub - 1)


    def send_chunk(i):
        span = slice(E * i, E * (i + 1))
        for c in range(NCLUS):
            high, low = pieces(integ[c, span, :])
            ihl[c, span, :] = jnp.concatenate([high, low], axis=1).astype(BF16)
            picked = lax.dot_general(
                esel[c], ihl[c, span, :], (((1,), (1,)), ((), ())), preferred_element_type=F32
            )
            for o in range(4):
                sbuf[i, o, SLOT * c : SLOT * (c + 1), :] = picked[SLOT * o : SLOT * (o + 1)]
            sbsub[i, SSUB * c : SSUB * (c + 1), :] = picked[4 * SLOT : 4 * SLOT + SSUB]
        for o in (0, 3, 1, 2):
            b = 3 - o
            copy = pltpu.make_async_remote_copy(
                src_ref=sbuf.at[i, o],
                dst_ref=gbuf.at[i, pl.ds(REG * b, REG), :],
                send_sem=send_sem.at[0],
                recv_sem=recv_sem.at[i],
                device_id=(regions[o], s),
                device_id_type=MESH,
            )
            copy.start()
        for d in range(1, n_sub):
            copy = pltpu.make_async_remote_copy(
                src_ref=sbsub.at[i],
                dst_ref=gbuf.at[i, pl.ds(4 * REG + SUB * (d - 1), SUB), :],
                send_sem=send_sem.at[1],
                recv_sem=recv_sem.at[i],
                device_id=(r, subs[d]),
                device_id_type=MESH,
            )
            copy.start()
        gbuf[i, FROM : FROM + SUB, :] = sbsub[i]

    k = NDER - 1
    for i, ps in enumerate(((0, 1, 2), (3, 4), (5, 6), (7, 8))):
        for p, x in zip(ps, apply_star(ps, ys)):
            for c in range(NCLUS):
                integ[c, M * p : M * (p + 1), :] += TAYLOR[c][k] * x
        send_chunk(i)

    for name in ("clus", "nbr", "orient", "vstiff", "lflux", "plus"):
        loads[name].wait()
    wstack[...] = left_stack(
        jnp.concatenate([vstiff[...].reshape(3 * M, M), -lflux[...].reshape(4 * M, M)], axis=0)
    )
    cl = clus[...]
    for group in groups:
        columns = []
        for q in group:
            span = slice(M * q, M * (q + 1))
            own = jnp.where(
                cl == 0, integ[0, span, :], jnp.where(cl == 1, integ[1, span, :], integ[2, span, :])
            )
            columns.append(right_stack(own))
        y = mm(wstack[...], jnp.concatenate(columns, axis=1))
        for i, q in enumerate(group):
            own_y[q] = y[:, E * i : E * (i + 1)]
    for ps in ((0, 1, 2), (3, 4, 5), (6, 7, 8)):
        acc = [state[p] for p in ps]
        for q in range(NQ):
            for j in range(7):
                y = own_y[q, M * j : M * (j + 1), :]
                for i, p in enumerate(ps):
                    weight = star[p, q, j : j + 1, :] if j < 3 else plus[p, q, j - 3 : j - 2, :]
                    acc[i] = acc[i] + weight * y
        for i, p in enumerate(ps):
            res[p] = acc[i]

    row_l = lax.broadcasted_iota(jnp.int32, (NCLUS * E, E), 0)
    row_g = lax.broadcasted_iota(jnp.int32, (512, E), 0)
    for f in range(4):
        v = nbr[f : f + 1, :]
        at_region = v - E
        at_sub = v - 2 * E
        k_region = (at_region >> 5) * REG + cl * SLOT + (at_region & 31)
        k_sub = 4 * REG + ((s - (at_sub >> 3) + 3) & 3) * SUB + cl * SSUB + (at_sub & 7)
        k_local = jnp.where(v < E, cl * E + v, -1)
        k_ghost = jnp.where(v < E, -1, jnp.where(v < 2 * E, k_region, k_sub))
        span = slice(E * f, E * (f + 1))
        ohl[:, span] = jnp.where(row_l == k_local, 1.0, 0.0).astype(BF16)
        ohg[:, span] = jnp.where(row_g == k_ghost, 1.0, 0.0).astype(BF16)

    for i in range(NCH):
        span = slice(E * i, E * (i + 1))
        high = jnp.concatenate([ihl[c, span, 0:E] for c in range(NCLUS)], axis=1)
        low = jnp.concatenate([ihl[c, span, E:] for c in range(NCLUS)], axis=1)
        part[i] = mm(jnp.concatenate([high, low], axis=0), ohl[...])

    loads["nflux"].wait()
    for f in range(4):
        for j in range(NORI // 2):
            pair = nflux[f, 2 * j : 2 * j + 2].reshape(2 * M, M)
            nstack[f, 2 * M * j : 2 * M * (j + 1), :] = left_stack(-pair)
    loads["minus"].wait()

    def whole(ref, sem):
        return pltpu.make_async_remote_copy(
            src_ref=ref, dst_ref=ref, send_sem=sem, recv_sem=sem, device_id=(regions[0], s), device_id_type=MESH
        )

    def arrived(ref, sem):
        whole(ref, sem).wait_recv()

    def left(ref, sem):
        whole(ref, sem).wait_send()

    def partner(h, q, f):
        got, row, end = [], M * q, M * (q + 1)
        while row < end:
            i = row // E
            stop = min(end, E * (i + 1))
            lo = row - E * i + E * h
            got.append(part[i, lo : lo + stop - row, E * f : E * (f + 1)])
            row = stop
        return got[0] if len(got) == 1 else jnp.concatenate(got, axis=0)

    todo = (((0, 1),), ((2, 3),), ((4, 5),), ((6, 7), (8,)))
    for i in range(NCH):
        arrived(gbuf.at[i, pl.ds(0, FROM), :], recv_sem.at[i])
        high, low = pieces(gbuf[i].T)
        part[i] += mm(jnp.concatenate([high, low], axis=0).astype(BF16), ohg[...])
        for group in todo[i]:
            for f in range(4):
                columns = [right_slots(partner(0, q, f), partner(1, q, f)) for q in group]
                every = mm(nstack[f], jnp.concatenate(columns, axis=1))
                face = orient[f : f + 1, :]
                for j in range(len(group)):
                    span = slice(E * j, E * (j + 1))
                    chosen = every[0:M, span]
                    for o in range(1, NORI):
                        chosen = jnp.where(face == o, every[M * o : M * (o + 1), span], chosen)
                    sel[len(group) * f + j] = chosen
            for ps in ((0, 1, 2), (3, 4, 5), (6, 7, 8)):
                acc = [res[p] for p in ps]
                for f in range(4):
                    for j, q in enumerate(group):
                        y = sel[len(group) * f + j]
                        for n, p in enumerate(ps):
                            acc[n] = acc[n] + minus[p, q, f : f + 1, :] * y
                for n, p in enumerate(ps):
                    res[p] = acc[n]

    left(sbuf, send_sem.at[0])
    left(gbuf.at[0, pl.ds(0, NCH * (n_sub - 1) * SUB), :], send_sem.at[1])


def local(n_region, n_sub, state, dstiff, vstiff, lflux, nflux, star, plus, minus, clus, nbr, orient, slist, blist):
    star, plus, minus = (jnp.transpose(a, (1, 2, 0, 3)) for a in (star, plus, minus))
    slist = jnp.transpose(slist, (0, 2, 1, 3)).reshape(NCLUS, 4, SLOT)
    blist = jnp.transpose(blist, (1, 0, 2))
    clus = clus.reshape(1, E)
    args = (state, dstiff, vstiff, lflux, nflux, star, plus, minus, clus, nbr, orient, slist, blist)
    vm = pltpu.VMEM
    return pl.pallas_call(
        functools.partial(body, n_region, n_sub),
        out_shape=pltpu.VMEM((NQ, M, E), F32),
        in_specs=[pl.BlockSpec(memory_space=pltpu.HBM)] * len(args),
        out_specs=pl.BlockSpec(memory_space=pltpu.VMEM),
        scratch_shapes=[vm(a.shape, a.dtype) for a in args]
        + [
            vm((3 * M, 256), BF16),
            vm((7 * M, 256), BF16),
            vm((4, NORI * M, 256), BF16),
            vm((NQ, 3 * M, E), F32),
            vm((NQ, 3 * M, E), F32),
            vm((NCLUS, ROWS, E), F32),
            vm((NCLUS, ROWS, 2 * E), BF16),
            vm((E, E), F32),
            vm((NCLUS, 144, 2 * E), BF16),
            vm((NCLUS * E, 4 * E), BF16),
            vm((512, 4 * E), BF16),
            vm((NQ, 7 * M, E), F32),
            vm((NCH, 2 * E, 4 * E), F32),
            vm((8, M, E), F32),
            vm((NCH, 4, REG, E), F32),
            vm((NCH, SUB, E), F32),
            vm((NCH, 512, E), F32),
            pltpu.SemaphoreType.DMA((len(args),)),
            pltpu.SemaphoreType.DMA((2,)),
            pltpu.SemaphoreType.DMA((NCH,)),
        ],
        compiler_params=pltpu.CompilerParams(
            collective_id=0, has_side_effects=True, vmem_limit_bytes=60 * 2**20
        ),
        cost_estimate=pl.CostEstimate(flops=2_000_000_000, bytes_accessed=4_000_000, transcendentals=0),
        name="ader_step",
    )(*args)


def solution(mesh):
    return jax.shard_map(
        functools.partial(local, mesh.shape["region"], mesh.shape["sub"]),
        mesh=mesh,
        in_specs=(
            P(None, None, ("region", "sub")),
            P(),
            P(),
            P(),
            P(),
            P(None, None, None, ("region", "sub")),
            P(None, None, None, ("region", "sub")),
            P(None, None, None, ("region", "sub")),
            P(("region", "sub")),
            P(None, ("region", "sub")),
            P(None, ("region", "sub")),
            P(("region", "sub"), None, None, None),
            P(("region", "sub"), None, None),
        ),
        out_specs=P(None, None, ("region", "sub")),
        check_vma=False,
    )
```

```python
import functools

import jax
import jax.numpy as jnp
from jax import lax
from jax.experimental import pallas as pl
from jax.experimental.pallas import tpu as pltpu
from jax.sharding import PartitionSpec as P

MESH = pl.DeviceIdType.MESH
F32, BF16 = jnp.float32, jnp.bfloat16

NDER = 6
NCLUS = 3
BASE_STEP = 0.25
OFFSETS = (-2, -1, 1, 2)
M = 56
NQ = 9
E = 128
SLOT = 32
SSUB = 8
NORI = 12
ROWS = 512
REG = NCLUS * SLOT
SUB = NCLUS * SSUB
FROM = 4 * REG + 3 * SUB
RING = 8
NCH = 4
TAYLOR = []
for _c in range(NCLUS):
    _factor, _row = 1.0, []
    for _k in range(NDER):
        _factor = _factor * (BASE_STEP * 2.0**_c) / (_k + 1)
        _row.append(_factor)
    TAYLOR.append(_row)


def pieces(x):
    high = x.astype(BF16).astype(F32)
    return high, x - high


def left_stack(a):
    high, low = pieces(a)
    gap = jnp.zeros((a.shape[0], 8), F32)
    return jnp.concatenate([high, gap, high, gap, low, gap, low, gap], axis=1).astype(BF16)


def right_slots(high, low):
    gap = jnp.zeros((8, high.shape[1]), F32)
    half = jnp.concatenate([high, gap, low, gap], axis=0).astype(BF16)
    return jnp.concatenate([half, half], axis=0)


def right_stack(x):
    return right_slots(*pieces(x))


def mm(a, b):
    return jnp.dot(a, b, preferred_element_type=F32)


def body(
    n_region, n_sub,
    state_h, dstiff_h, vstiff_h, lflux_h, nflux_h, star_h, plus_h, minus_h,
    clus_h, nbr_h, orient_h, slist_h, blist_h,
    res,
    state, dstiff, vstiff, lflux, nflux, star, plus, minus, clus, nbr, orient, slist, blist,
    dstack, wstack, nstack, ys, ys2, integ, ihl, tmp, esel, ohl, ohg, own_y, part, sel,
    sbuf, sbsub, gbuf,
    in_sem, send_sem, recv_sem,
):
    r = lax.axis_index("region")
    s = lax.axis_index("sub")
    regions = [lax.rem(r + (o + n_region), n_region) for o in OFFSETS]
    subs = [lax.rem(s + d, n_sub) for d in range(n_sub)]
    last = (r + 1) // n_region
    via = min(2 * RING, n_region // 2 + 1) - 1

    barrier = pltpu.get_barrier_semaphore()
    for j in regions:
        pl.semaphore_signal(barrier, inc=1, device_id=(j, s), device_id_type=MESH)
    for d in range(1, n_sub):
        pl.semaphore_signal(barrier, inc=1, device_id=(r, subs[d]), device_id_type=MESH)

    @pl.when(r == via)
    def _():
        pl.semaphore_signal(barrier, inc=1, device_id=(n_region - 1, s), device_id_type=MESH)

    @pl.when(r == 0)
    def _():
        pl.semaphore_signal(barrier, inc=1, device_id=(via, s), device_id_type=MESH)

    loads = {}
    for i, (name, src, dst) in enumerate((
        ("dstiff", dstiff_h, dstiff), ("state", state_h, state), ("star", star_h, star),
        ("slist", slist_h, slist), ("blist", blist_h, blist),
        ("vstiff", vstiff_h, vstiff),
        ("clus", clus_h, clus), ("nbr", nbr_h, nbr), ("orient", orient_h, orient),
        ("lflux", lflux_h, lflux), ("plus", plus_h, plus), ("nflux", nflux_h, nflux),
        ("minus", minus_h, minus),
    )):
        loads[name] = pltpu.make_async_copy(src, dst, in_sem.at[i])
        if i < 5:
            loads[name].start()

    late = ("vstiff", "clus", "nbr", "orient", "lflux", "plus", "nflux", "minus")
    groups = ((0, 1), (2, 3), (4, 5), (6, 7), (8,))

    integ[:, NQ * M :, :] = jnp.zeros((NCLUS, ROWS - NQ * M, E), F32)
    gbuf[0:NCH, 4 * REG + n_sub * SUB :, :] = jnp.zeros((NCH, 512 - 4 * REG - n_sub * SUB, E), F32)

    loads["dstiff"].wait()
    dstack[...] = left_stack(-dstiff[...].reshape(3 * M, M))

    loads["state"].wait()

    pairs = ((0, 1), (2, 3), (4, 5), (6, 7), (8,))

    def modes(group, values, target):
        y = mm(dstack[...], jnp.concatenate([right_stack(x) for x in values], axis=1))
        for i, q in enumerate(group):
            target[q] = y[:, E * i : E * (i + 1)]

    for group in pairs:
        modes(group, [state[q] for q in group], ys)
    for q in range(NQ):
        x = state[q]
        for c in range(NCLUS):
            integ[c, M * q : M * (q + 1), :] = TAYLOR[c][0] * x

    def apply_star(ps, source):
        acc = [None] * len(ps)
        for q in range(NQ):
            for d in range(3):
                y = source[q, M * d : M * (d + 1), :]
                for i, p in enumerate(ps):
                    term = star[p, q, d : d + 1, :] * y
                    acc[i] = term if acc[i] is None else acc[i] + term
        return acc

    loads["slist"].wait()
    loads["blist"].wait()
    tmp[...] = jnp.zeros((E, E), F32)
    for c in range(NCLUS):
        tmp[8 * c : 8 * c + 4, 0:SLOT] = slist[c].astype(F32)
        tmp[8 * c + 4 : 8 * c + 5, 0:SSUB] = blist[c].astype(F32)
    lists = tmp[...].T
    lane = lax.broadcasted_iota(jnp.int32, (SLOT, E), 1).astype(F32)
    for c in range(NCLUS):
        rows = [
            jnp.where(lists[0:SLOT, 8 * c + o : 8 * c + o + 1] == lane, 1.0, 0.0) for o in range(4)
        ]
        rows.append(jnp.where(lists[0:SSUB, 8 * c + 4 : 8 * c + 5] == lane[0:SSUB], 1.0, 0.0))
        rows.append(jnp.zeros((8, E), F32))
        onehot = jnp.concatenate(rows, axis=0).astype(BF16)
        esel[c] = jnp.concatenate([onehot, onehot], axis=1)

    loads["star"].wait()
    for name in late:
        loads[name].start()

    def step(k, source, target):
        weights = []
        for c in range(NCLUS):
            weights.append(TAYLOR[c][k])
        for group in ((0, 1, 2), (3, 4, 5), (6, 7, 8)):
            xs = apply_star(group, source)
            modes(group, xs, target)
            for p, x in zip(group, xs):
                for c in range(NCLUS):
                    integ[c, M * p : M * (p + 1), :] += weights[c] * x

    def two_steps(n, carry):
        step(2 * n + 1, ys, ys2)
        step(2 * n + 2, ys2, ys)
        return carry

    two_steps(0, 0)
    two_steps(1, 0)

    pl.semaphore_wait(barrier, 4 + n_sub - 1 + jnp.where((r == via) | (r == n_region - 1), 1, 0))


    def send_chunk(i):
        span = slice(E * i, E * (i + 1))
        for c in range(NCLUS):
            high, low = pieces(integ[c, span, :])
            ihl[c, span, :] = jnp.concatenate([high, low], axis=1).astype(BF16)
            picked = lax.dot_general(
                esel[c], ihl[c, span, :], (((1,), (1,)), ((), ())), preferred_element_type=F32
            )
            for o in range(4):
                sbuf[i, o, SLOT * c : SLOT * (c + 1), :] = picked[SLOT * o : SLOT * (o + 1)]
            sbsub[i, SSUB * c : SSUB * (c + 1), :] = picked[4 * SLOT : 4 * SLOT + SSUB]
        for o in (0, 3, 1, 2):
            b = 3 - o
            slot, target = (i + NCH * last, regions[o] + via * last) if o == 2 else (i, regions[o])
            pltpu.make_async_remote_copy(
                src_ref=sbuf.at[i, o],
                dst_ref=gbuf.at[slot, pl.ds(REG * b, REG), :],
                send_sem=send_sem.at[0],
                recv_sem=recv_sem.at[slot],
                device_id=(target, s),
                device_id_type=MESH,
            ).start()
        for d in range(1, n_sub):
            copy = pltpu.make_async_remote_copy(
                src_ref=sbsub.at[i],
                dst_ref=gbuf.at[i, pl.ds(4 * REG + SUB * (d - 1), SUB), :],
                send_sem=send_sem.at[1],
                recv_sem=recv_sem.at[i],
                device_id=(r, subs[d]),
                device_id_type=MESH,
            )
            copy.start()
        gbuf[i, FROM : FROM + SUB, :] = sbsub[i]

    k = NDER - 1
    for i, ps in enumerate(((0, 1, 2), (3, 4), (5, 6), (7, 8))):
        for p, x in zip(ps, apply_star(ps, ys)):
            for c in range(NCLUS):
                integ[c, M * p : M * (p + 1), :] += TAYLOR[c][k] * x
        send_chunk(i)

    for name in ("clus", "nbr", "orient", "vstiff", "lflux", "plus"):
        loads[name].wait()
    wstack[...] = left_stack(
        jnp.concatenate([vstiff[...].reshape(3 * M, M), -lflux[...].reshape(4 * M, M)], axis=0)
    )
    cl = clus[...]
    for group in groups:
        columns = []
        for q in group:
            span = slice(M * q, M * (q + 1))
            own = jnp.where(
                cl == 0, integ[0, span, :], jnp.where(cl == 1, integ[1, span, :], integ[2, span, :])
            )
            columns.append(right_stack(own))
        y = mm(wstack[...], jnp.concatenate(columns, axis=1))
        for i, q in enumerate(group):
            own_y[q] = y[:, E * i : E * (i + 1)]
    for ps in ((0, 1, 2), (3, 4, 5), (6, 7, 8)):
        acc = [state[p] for p in ps]
        for q in range(NQ):
            for j in range(7):
                y = own_y[q, M * j : M * (j + 1), :]
                for i, p in enumerate(ps):
                    weight = star[p, q, j : j + 1, :] if j < 3 else plus[p, q, j - 3 : j - 2, :]
                    acc[i] = acc[i] + weight * y
        for i, p in enumerate(ps):
            res[p] = acc[i]

    row_l = lax.broadcasted_iota(jnp.int32, (NCLUS * E, E), 0)
    row_g = lax.broadcasted_iota(jnp.int32, (512, E), 0)
    for f in range(4):
        v = nbr[f : f + 1, :]
        at_region = v - E
        at_sub = v - 2 * E
        k_region = (at_region >> 5) * REG + cl * SLOT + (at_region & 31)
        k_sub = 4 * REG + ((s - (at_sub >> 3) + 3) & 3) * SUB + cl * SSUB + (at_sub & 7)
        k_local = jnp.where(v < E, cl * E + v, -1)
        k_ghost = jnp.where(v < E, -1, jnp.where(v < 2 * E, k_region, k_sub))
        span = slice(E * f, E * (f + 1))
        ohl[:, span] = jnp.where(row_l == k_local, 1.0, 0.0).astype(BF16)
        ohg[:, span] = jnp.where(row_g == k_ghost, 1.0, 0.0).astype(BF16)

    for i in range(NCH):
        span = slice(E * i, E * (i + 1))
        high = jnp.concatenate([ihl[c, span, 0:E] for c in range(NCLUS)], axis=1)
        low = jnp.concatenate([ihl[c, span, E:] for c in range(NCLUS)], axis=1)
        part[i] = mm(jnp.concatenate([high, low], axis=0), ohl[...])

    loads["nflux"].wait()
    for f in range(4):
        for j in range(NORI // 2):
            pair = nflux[f, 2 * j : 2 * j + 2].reshape(2 * M, M)
            nstack[f, 2 * M * j : 2 * M * (j + 1), :] = left_stack(-pair)
    loads["minus"].wait()

    def whole(ref, sem):
        return pltpu.make_async_remote_copy(
            src_ref=ref, dst_ref=ref, send_sem=sem, recv_sem=sem, device_id=(regions[0], s), device_id_type=MESH
        )

    def arrived(ref, sem):
        whole(ref, sem).wait_recv()

    def left(ref, sem):
        whole(ref, sem).wait_send()

    @pl.when(r == via)
    def _():
        span = pl.ds(REG, REG)
        for i in range(NCH):
            arrived(gbuf.at[NCH + i, span, :], recv_sem.at[NCH + i])
            pltpu.make_async_remote_copy(
                src_ref=gbuf.at[NCH + i, span, :],
                dst_ref=gbuf.at[i, span, :],
                send_sem=send_sem.at[2],
                recv_sem=recv_sem.at[i],
                device_id=(0, s),
                device_id_type=MESH,
            ).start()
        left(gbuf.at[0, pl.ds(0, NCH * REG), :], send_sem.at[2])

    def partner(h, q, f):
        got, row, end = [], M * q, M * (q + 1)
        while row < end:
            i = row // E
            stop = min(end, E * (i + 1))
            lo = row - E * i + E * h
            got.append(part[i, lo : lo + stop - row, E * f : E * (f + 1)])
            row = stop
        return got[0] if len(got) == 1 else jnp.concatenate(got, axis=0)

    todo = (((0, 1),), ((2, 3),), ((4, 5),), ((6, 7), (8,)))
    for i in range(NCH):
        arrived(gbuf.at[i, pl.ds(0, FROM), :], recv_sem.at[i])
        high, low = pieces(gbuf[i].T)
        part[i] += mm(jnp.concatenate([high, low], axis=0).astype(BF16), ohg[...])
        for group in todo[i]:
            for f in range(4):
                columns = [right_slots(partner(0, q, f), partner(1, q, f)) for q in group]
                every = mm(nstack[f], jnp.concatenate(columns, axis=1))
                face = orient[f : f + 1, :]
                for j in range(len(group)):
                    span = slice(E * j, E * (j + 1))
                    chosen = every[0:M, span]
                    for o in range(1, NORI):
                        chosen = jnp.where(face == o, every[M * o : M * (o + 1), span], chosen)
                    sel[len(group) * f + j] = chosen
            for ps in ((0, 1, 2), (3, 4, 5), (6, 7, 8)):
                acc = [res[p] for p in ps]
                for f in range(4):
                    for j, q in enumerate(group):
                        y = sel[len(group) * f + j]
                        for n, p in enumerate(ps):
                            acc[n] = acc[n] + minus[p, q, f : f + 1, :] * y
                for n, p in enumerate(ps):
                    res[p] = acc[n]

    left(sbuf, send_sem.at[0])
    left(gbuf.at[0, pl.ds(0, NCH * (n_sub - 1) * SUB), :], send_sem.at[1])


def local(n_region, n_sub, state, dstiff, vstiff, lflux, nflux, star, plus, minus, clus, nbr, orient, slist, blist):
    star, plus, minus = (jnp.transpose(a, (1, 2, 0, 3)) for a in (star, plus, minus))
    slist = jnp.transpose(slist, (0, 2, 1, 3)).reshape(NCLUS, 4, SLOT)
    blist = jnp.transpose(blist, (1, 0, 2))
    clus = clus.reshape(1, E)
    args = (state, dstiff, vstiff, lflux, nflux, star, plus, minus, clus, nbr, orient, slist, blist)
    vm = pltpu.VMEM
    return pl.pallas_call(
        functools.partial(body, n_region, n_sub),
        out_shape=pltpu.VMEM((NQ, M, E), F32),
        in_specs=[pl.BlockSpec(memory_space=pltpu.HBM)] * len(args),
        out_specs=pl.BlockSpec(memory_space=pltpu.VMEM),
        scratch_shapes=[vm(a.shape, a.dtype) for a in args]
        + [
            vm((3 * M, 256), BF16),
            vm((7 * M, 256), BF16),
            vm((4, NORI * M, 256), BF16),
            vm((NQ, 3 * M, E), F32),
            vm((NQ, 3 * M, E), F32),
            vm((NCLUS, ROWS, E), F32),
            vm((NCLUS, ROWS, 2 * E), BF16),
            vm((E, E), F32),
            vm((NCLUS, 144, 2 * E), BF16),
            vm((NCLUS * E, 4 * E), BF16),
            vm((512, 4 * E), BF16),
            vm((NQ, 7 * M, E), F32),
            vm((NCH, 2 * E, 4 * E), F32),
            vm((8, M, E), F32),
            vm((NCH, 4, REG, E), F32),
            vm((NCH, SUB, E), F32),
            vm((2 * NCH, 512, E), F32),
            pltpu.SemaphoreType.DMA((len(args),)),
            pltpu.SemaphoreType.DMA((3,)),
            pltpu.SemaphoreType.DMA((2 * NCH,)),
        ],
        compiler_params=pltpu.CompilerParams(
            collective_id=0, has_side_effects=True, vmem_limit_bytes=60 * 2**20
        ),
        cost_estimate=pl.CostEstimate(flops=2_000_000_000, bytes_accessed=4_000_000, transcendentals=0),
        name="ader_step",
    )(*args)


def solution(mesh):
    return jax.shard_map(
        functools.partial(local, mesh.shape["region"], mesh.shape["sub"]),
        mesh=mesh,
        in_specs=(
            P(None, None, ("region", "sub")),
            P(),
            P(),
            P(),
            P(),
            P(None, None, None, ("region", "sub")),
            P(None, None, None, ("region", "sub")),
            P(None, None, None, ("region", "sub")),
            P(("region", "sub")),
            P(None, ("region", "sub")),
            P(None, ("region", "sub")),
            P(("region", "sub"), None, None, None),
            P(("region", "sub"), None, None),
        ),
        out_specs=P(None, None, ("region", "sub")),
        check_vma=False,
    )
```

```python
import functools

import jax
import jax.numpy as jnp
from jax import lax
from jax.experimental import pallas as pl
from jax.experimental.pallas import tpu as pltpu
from jax.sharding import PartitionSpec as P

MESH = pl.DeviceIdType.MESH
F32, BF16 = jnp.float32, jnp.bfloat16

NDER = 6
NCLUS = 3
BASE_STEP = 0.25
OFFSETS = (-2, -1, 1, 2)
M = 56
NQ = 9
E = 128
SLOT = 32
SSUB = 8
NORI = 12
ROWS = 512
REG = NCLUS * SLOT
SUB = NCLUS * SSUB
FROM = 4 * REG + 3 * SUB
RING = 8
NCH = 4
TAYLOR = []
for _c in range(NCLUS):
    _factor, _row = 1.0, []
    for _k in range(NDER):
        _factor = _factor * (BASE_STEP * 2.0**_c) / (_k + 1)
        _row.append(_factor)
    TAYLOR.append(_row)


def pieces(x):
    high = x.astype(BF16).astype(F32)
    return high, x - high


def left_stack(a):
    high, low = pieces(a)
    gap = jnp.zeros((a.shape[0], 8), F32)
    return jnp.concatenate([high, gap, high, gap, low, gap, low, gap], axis=1).astype(BF16)


def right_slots(high, low):
    gap = jnp.zeros((8, high.shape[1]), F32)
    half = jnp.concatenate([high, gap, low, gap], axis=0).astype(BF16)
    return jnp.concatenate([half, half], axis=0)


def right_stack(x):
    return right_slots(*pieces(x))


def mm(a, b):
    return jnp.dot(a, b, preferred_element_type=F32)


def body(
    n_region, n_sub,
    state_h, dstiff_h, vstiff_h, lflux_h, nflux_h, star_h, plus_h, minus_h,
    clus_h, nbr_h, orient_h, slist_h, blist_h,
    res,
    state, dstiff, vstiff, lflux, nflux, star, plus, minus, clus, nbr, orient, slist, blist,
    dstack, wstack, nstack, ys, ys2, integ, ihl, tmp, esel, ohl, ohg, own_y, part, sel,
    sbuf, sbsub, gbuf,
    in_sem, send_sem, recv_sem,
):
    r = lax.axis_index("region")
    s = lax.axis_index("sub")
    regions = [lax.rem(r + (o + n_region), n_region) for o in OFFSETS]
    subs = [lax.rem(s + d, n_sub) for d in range(n_sub)]
    last = (r + 1) // n_region
    via = min(2 * RING, n_region // 2 + 1) - 1

    barrier = pltpu.get_barrier_semaphore()
    for j in regions:
        pl.semaphore_signal(barrier, inc=1, device_id=(j, s), device_id_type=MESH)
    for d in range(1, n_sub):
        pl.semaphore_signal(barrier, inc=1, device_id=(r, subs[d]), device_id_type=MESH)

    @pl.when(r == via)
    def _():
        pl.semaphore_signal(barrier, inc=1, device_id=(n_region - 1, s), device_id_type=MESH)

    @pl.when(r == 0)
    def _():
        pl.semaphore_signal(barrier, inc=1, device_id=(via, s), device_id_type=MESH)

    loads = {}
    for i, (name, src, dst) in enumerate((
        ("dstiff", dstiff_h, dstiff), ("state", state_h, state), ("star", star_h, star),
        ("slist", slist_h, slist), ("blist", blist_h, blist),
        ("vstiff", vstiff_h, vstiff),
        ("clus", clus_h, clus), ("nbr", nbr_h, nbr), ("orient", orient_h, orient),
        ("lflux", lflux_h, lflux), ("plus", plus_h, plus), ("nflux", nflux_h, nflux),
        ("minus", minus_h, minus),
    )):
        loads[name] = pltpu.make_async_copy(src, dst, in_sem.at[i])
        if i < 5:
            loads[name].start()

    late = ("vstiff", "clus", "nbr", "orient", "lflux", "plus", "nflux", "minus")
    groups = ((0, 1), (2, 3), (4, 5), (6, 7), (8,))

    integ[:, NQ * M :, :] = jnp.zeros((NCLUS, ROWS - NQ * M, E), F32)
    gbuf[0:NCH, 4 * REG + n_sub * SUB :, :] = jnp.zeros((NCH, 512 - 4 * REG - n_sub * SUB, E), F32)

    loads["dstiff"].wait()
    dstack[...] = left_stack(-dstiff[...].reshape(3 * M, M))

    loads["state"].wait()

    pairs = ((0, 1), (2, 3), (4, 5), (6, 7), (8,))

    def modes(group, values, target):
        y = mm(dstack[...], jnp.concatenate([right_stack(x) for x in values], axis=1))
        for i, q in enumerate(group):
            target[q] = y[:, E * i : E * (i + 1)]

    for group in pairs:
        modes(group, [state[q] for q in group], ys)
    for q in range(NQ):
        x = state[q]
        for c in range(NCLUS):
            integ[c, M * q : M * (q + 1), :] = TAYLOR[c][0] * x

    def apply_star(ps, source):
        acc = [None] * len(ps)
        for q in range(NQ):
            for d in range(3):
                y = source[q, M * d : M * (d + 1), :]
                for i, p in enumerate(ps):
                    term = star[p, q, d : d + 1, :] * y
                    acc[i] = term if acc[i] is None else acc[i] + term
        return acc

    loads["slist"].wait()
    loads["blist"].wait()
    tmp[...] = jnp.zeros((E, E), F32)
    for c in range(NCLUS):
        tmp[8 * c : 8 * c + 4, 0:SLOT] = slist[c].astype(F32)
        tmp[8 * c + 4 : 8 * c + 5, 0:SSUB] = blist[c].astype(F32)
    lists = tmp[...].T
    lane = lax.broadcasted_iota(jnp.int32, (SLOT, E), 1).astype(F32)
    for c in range(NCLUS):
        rows = [
            jnp.where(lists[0:SLOT, 8 * c + o : 8 * c + o + 1] == lane, 1.0, 0.0) for o in range(4)
        ]
        rows.append(jnp.where(lists[0:SSUB, 8 * c + 4 : 8 * c + 5] == lane[0:SSUB], 1.0, 0.0))
        rows.append(jnp.zeros((8, E), F32))
        onehot = jnp.concatenate(rows, axis=0).astype(BF16)
        esel[c] = jnp.concatenate([onehot, onehot], axis=1)

    loads["star"].wait()
    for name in late:
        loads[name].start()

    def step(k, source, target):
        weights = []
        for c in range(NCLUS):
            weights.append(TAYLOR[c][k])
        for group in ((0, 1, 2), (3, 4, 5), (6, 7, 8)):
            xs = apply_star(group, source)
            modes(group, xs, target)
            for p, x in zip(group, xs):
                for c in range(NCLUS):
                    integ[c, M * p : M * (p + 1), :] += weights[c] * x

    def two_steps(n, carry):
        step(2 * n + 1, ys, ys2)
        step(2 * n + 2, ys2, ys)
        return carry

    two_steps(0, 0)
    two_steps(1, 0)

    pl.semaphore_wait(barrier, 4 + n_sub - 1 + jnp.where((r == via) | (r == n_region - 1), 1, 0))


    def send_chunk(i):
        span = slice(E * i, E * (i + 1))
        for c in range(NCLUS):
            high, low = pieces(integ[c, span, :])
            ihl[c, span, :] = jnp.concatenate([high, low], axis=1).astype(BF16)
            picked = lax.dot_general(
                esel[c], ihl[c, span, :], (((1,), (1,)), ((), ())), preferred_element_type=F32
            )
            for o in range(4):
                sbuf[i, o, SLOT * c : SLOT * (c + 1), :] = picked[SLOT * o : SLOT * (o + 1)]
            sbsub[i, SSUB * c : SSUB * (c + 1), :] = picked[4 * SLOT : 4 * SLOT + SSUB]
        for o in (2, 3, 0, 1):
            b = 3 - o
            slot, target = (i + NCH * last, regions[o] + via * last) if o == 2 else (i, regions[o])
            pltpu.make_async_remote_copy(
                src_ref=sbuf.at[i, o],
                dst_ref=gbuf.at[slot, pl.ds(REG * b, REG), :],
                send_sem=send_sem.at[0],
                recv_sem=recv_sem.at[slot],
                device_id=(target, s),
                device_id_type=MESH,
            ).start()
        for d in range(1, n_sub):
            copy = pltpu.make_async_remote_copy(
                src_ref=sbsub.at[i],
                dst_ref=gbuf.at[i, pl.ds(4 * REG + SUB * (d - 1), SUB), :],
                send_sem=send_sem.at[1],
                recv_sem=recv_sem.at[i],
                device_id=(r, subs[d]),
                device_id_type=MESH,
            )
            copy.start()
        gbuf[i, FROM : FROM + SUB, :] = sbsub[i]

    k = NDER - 1
    for i, ps in enumerate(((0, 1, 2), (3, 4), (5, 6), (7, 8))):
        for p, x in zip(ps, apply_star(ps, ys)):
            for c in range(NCLUS):
                integ[c, M * p : M * (p + 1), :] += TAYLOR[c][k] * x
        send_chunk(i)

    for name in ("clus", "nbr", "orient", "vstiff", "lflux", "plus"):
        loads[name].wait()
    wstack[...] = left_stack(
        jnp.concatenate([vstiff[...].reshape(3 * M, M), -lflux[...].reshape(4 * M, M)], axis=0)
    )
    cl = clus[...]
    for group in groups:
        columns = []
        for q in group:
            span = slice(M * q, M * (q + 1))
            own = jnp.where(
                cl == 0, integ[0, span, :], jnp.where(cl == 1, integ[1, span, :], integ[2, span, :])
            )
            columns.append(right_stack(own))
        y = mm(wstack[...], jnp.concatenate(columns, axis=1))
        for i, q in enumerate(group):
            own_y[q] = y[:, E * i : E * (i + 1)]
    for ps in ((0, 1, 2), (3, 4, 5), (6, 7, 8)):
        acc = [state[p] for p in ps]
        for q in range(NQ):
            for j in range(7):
                y = own_y[q, M * j : M * (j + 1), :]
                for i, p in enumerate(ps):
                    weight = star[p, q, j : j + 1, :] if j < 3 else plus[p, q, j - 3 : j - 2, :]
                    acc[i] = acc[i] + weight * y
        for i, p in enumerate(ps):
            res[p] = acc[i]

    row_l = lax.broadcasted_iota(jnp.int32, (NCLUS * E, E), 0)
    row_g = lax.broadcasted_iota(jnp.int32, (512, E), 0)
    for f in range(4):
        v = nbr[f : f + 1, :]
        at_region = v - E
        at_sub = v - 2 * E
        k_region = (at_region >> 5) * REG + cl * SLOT + (at_region & 31)
        k_sub = 4 * REG + ((s - (at_sub >> 3) + 3) & 3) * SUB + cl * SSUB + (at_sub & 7)
        k_local = jnp.where(v < E, cl * E + v, -1)
        k_ghost = jnp.where(v < E, -1, jnp.where(v < 2 * E, k_region, k_sub))
        span = slice(E * f, E * (f + 1))
        ohl[:, span] = jnp.where(row_l == k_local, 1.0, 0.0).astype(BF16)
        ohg[:, span] = jnp.where(row_g == k_ghost, 1.0, 0.0).astype(BF16)

    for i in range(NCH):
        span = slice(E * i, E * (i + 1))
        high = jnp.concatenate([ihl[c, span, 0:E] for c in range(NCLUS)], axis=1)
        low = jnp.concatenate([ihl[c, span, E:] for c in range(NCLUS)], axis=1)
        part[i] = mm(jnp.concatenate([high, low], axis=0), ohl[...])

    loads["nflux"].wait()
    for f in range(4):
        for j in range(NORI // 2):
            pair = nflux[f, 2 * j : 2 * j + 2].reshape(2 * M, M)
            nstack[f, 2 * M * j : 2 * M * (j + 1), :] = left_stack(-pair)
    loads["minus"].wait()

    def whole(ref, sem):
        return pltpu.make_async_remote_copy(
            src_ref=ref, dst_ref=ref, send_sem=sem, recv_sem=sem, device_id=(regions[0], s), device_id_type=MESH
        )

    def arrived(ref, sem):
        whole(ref, sem).wait_recv()

    def left(ref, sem):
        whole(ref, sem).wait_send()

    @pl.when(r == via)
    def _():
        span = pl.ds(REG, REG)
        for i in range(NCH):
            arrived(gbuf.at[NCH + i, span, :], recv_sem.at[NCH + i])
            pltpu.make_async_remote_copy(
                src_ref=gbuf.at[NCH + i, span, :],
                dst_ref=gbuf.at[i, span, :],
                send_sem=send_sem.at[2],
                recv_sem=recv_sem.at[i],
                device_id=(0, s),
                device_id_type=MESH,
            ).start()
        left(gbuf.at[0, pl.ds(0, NCH * REG), :], send_sem.at[2])

    def partner(h, q, f):
        got, row, end = [], M * q, M * (q + 1)
        while row < end:
            i = row // E
            stop = min(end, E * (i + 1))
            lo = row - E * i + E * h
            got.append(part[i, lo : lo + stop - row, E * f : E * (f + 1)])
            row = stop
        return got[0] if len(got) == 1 else jnp.concatenate(got, axis=0)

    todo = (((0, 1),), ((2, 3),), ((4, 5),), ((6, 7), (8,)))
    for i in range(NCH):
        arrived(gbuf.at[i, pl.ds(0, FROM), :], recv_sem.at[i])
        high, low = pieces(gbuf[i].T)
        part[i] += mm(jnp.concatenate([high, low], axis=0).astype(BF16), ohg[...])
        for group in todo[i]:
            for f in range(4):
                columns = [right_slots(partner(0, q, f), partner(1, q, f)) for q in group]
                every = mm(nstack[f], jnp.concatenate(columns, axis=1))
                face = orient[f : f + 1, :]
                for j in range(len(group)):
                    span = slice(E * j, E * (j + 1))
                    chosen = every[0:M, span]
                    for o in range(1, NORI):
                        chosen = jnp.where(face == o, every[M * o : M * (o + 1), span], chosen)
                    sel[len(group) * f + j] = chosen
            for ps in ((0, 1, 2), (3, 4, 5), (6, 7, 8)):
                acc = [res[p] for p in ps]
                for f in range(4):
                    for j, q in enumerate(group):
                        y = sel[len(group) * f + j]
                        for n, p in enumerate(ps):
                            acc[n] = acc[n] + minus[p, q, f : f + 1, :] * y
                for n, p in enumerate(ps):
                    res[p] = acc[n]

    left(sbuf, send_sem.at[0])
    left(gbuf.at[0, pl.ds(0, NCH * (n_sub - 1) * SUB), :], send_sem.at[1])


def local(n_region, n_sub, state, dstiff, vstiff, lflux, nflux, star, plus, minus, clus, nbr, orient, slist, blist):
    star, plus, minus = (jnp.transpose(a, (1, 2, 0, 3)) for a in (star, plus, minus))
    slist = jnp.transpose(slist, (0, 2, 1, 3)).reshape(NCLUS, 4, SLOT)
    blist = jnp.transpose(blist, (1, 0, 2))
    clus = clus.reshape(1, E)
    args = (state, dstiff, vstiff, lflux, nflux, star, plus, minus, clus, nbr, orient, slist, blist)
    vm = pltpu.VMEM
    return pl.pallas_call(
        functools.partial(body, n_region, n_sub),
        out_shape=pltpu.VMEM((NQ, M, E), F32),
        in_specs=[pl.BlockSpec(memory_space=pltpu.HBM)] * len(args),
        out_specs=pl.BlockSpec(memory_space=pltpu.VMEM),
        scratch_shapes=[vm(a.shape, a.dtype) for a in args]
        + [
            vm((3 * M, 256), BF16),
            vm((7 * M, 256), BF16),
            vm((4, NORI * M, 256), BF16),
            vm((NQ, 3 * M, E), F32),
            vm((NQ, 3 * M, E), F32),
            vm((NCLUS, ROWS, E), F32),
            vm((NCLUS, ROWS, 2 * E), BF16),
            vm((E, E), F32),
            vm((NCLUS, 144, 2 * E), BF16),
            vm((NCLUS * E, 4 * E), BF16),
            vm((512, 4 * E), BF16),
            vm((NQ, 7 * M, E), F32),
            vm((NCH, 2 * E, 4 * E), F32),
            vm((8, M, E), F32),
            vm((NCH, 4, REG, E), F32),
            vm((NCH, SUB, E), F32),
            vm((2 * NCH, 512, E), F32),
            pltpu.SemaphoreType.DMA((len(args),)),
            pltpu.SemaphoreType.DMA((3,)),
            pltpu.SemaphoreType.DMA((2 * NCH,)),
        ],
        compiler_params=pltpu.CompilerParams(
            collective_id=0, has_side_effects=True, vmem_limit_bytes=60 * 2**20
        ),
        cost_estimate=pl.CostEstimate(flops=2_000_000_000, bytes_accessed=4_000_000, transcendentals=0),
        name="ader_step",
    )(*args)


def solution(mesh):
    return jax.shard_map(
        functools.partial(local, mesh.shape["region"], mesh.shape["sub"]),
        mesh=mesh,
        in_specs=(
            P(None, None, ("region", "sub")),
            P(),
            P(),
            P(),
            P(),
            P(None, None, None, ("region", "sub")),
            P(None, None, None, ("region", "sub")),
            P(None, None, None, ("region", "sub")),
            P(("region", "sub")),
            P(None, ("region", "sub")),
            P(None, ("region", "sub")),
            P(("region", "sub"), None, None, None),
            P(("region", "sub"), None, None),
        ),
        out_specs=P(None, None, ("region", "sub")),
        check_vma=False,
    )
```
